1024 devices in a mesh: blk: 16 (over z_hi, x, core), ulysses: 64 (over y, z_lo).
Axes of the slice: x: 4, y: 8, z: 16 (z_hi: 2, z_lo: 8; z = z_hi * 8 + z_lo), core: 2. Of those that a mesh axis runs over, the one named last changes fastest.
Arguments:
- query_rows: bfloat16 [32, 131072, 128], P(None, ('blk', 'ulysses')), may hold values from -160 to 160
- out_grad: bfloat16 [32, 131072, 128], P(None, ('blk', 'ulysses')), may hold values from -6 to 6
- key_rows: bfloat16 [32, 2048, 128], P(None, 'blk'), may hold values from -6 to 6
- value_rows: bfloat16 [32, 2048, 128], P(None, 'blk'), may hold values from -6 to 6
- routes: int32 [16, 16], replicated, may hold values from 0 to 7
Outputs:
- query_grad: bfloat16 [32, 131072, 128], P(None, ('blk', 'ulysses'))
- key_grad: float32 [32, 2048, 128], P(None, ('blk', 'ulysses'))
- value_grad: float32 [32, 2048, 128], P(None, ('blk', 'ulysses'))
The draws below stay inside these ranges and needn't reach their ends.
All inputs are finite; a program needn't handle non-finite values.
Results may differ from the reference program's by a relative error of at most 0.0056.
Values may be sent and summed in bfloat16 or wider, within the bound.
A program may use at most 32 MiB of HBM per device.

```python
import math
import jax
import jax.numpy as jnp
from jax import lax

H = 32
HD = 128
TOK_DEV = 128
KB = 16
KBLOCKS = 8
KG = 128
QS = 2
TQB = 64
TOKENS = 131072
KEYS = 2048
NK = 384
N_BLK = 16
N_ULYSSES = 64


def key_table(key):
    normal_draw = jax.random.truncated_normal(jax.random.fold_in(key, 11), -6.0, 6.0, (H, KEYS, HD), jnp.float32)
    return normal_draw


def draw_key_rows(key, part):
    normal_draw = key_table(key)
    return normal_draw.astype(jnp.bfloat16)


def draw_query_rows(key, part):
    normal_draw = jax.random.truncated_normal(jax.random.fold_in(key, 17), -6.0, 6.0, (H, TOKENS, HD), jnp.float32)
    return normal_draw.astype(jnp.bfloat16)


def place_ends(values, stream_key, smallest, largest):
    index_at = [jax.random.randint(jax.random.fold_in(stream_key, axis), (), 0, length) for axis, length in enumerate(values.shape)]
    main_axis = values.shape.index(max(values.shape))
    next_to = index_at[:main_axis] + [(index_at[main_axis] + 1) % values.shape[main_axis]] + index_at[main_axis + 1:]
    return values.at[tuple(index_at)].set(smallest).at[tuple(next_to)].set(largest)


def block_levels(own_key, extent, shards, smallest, largest):
    level = 1.0
    for dim, shards_of in shards:
        draws = jax.random.uniform(jax.random.fold_in(jax.random.fold_in(own_key, 6), dim), (shards_of,), jnp.float32, smallest / len(shards), largest / len(shards))
        level = level * jnp.repeat(jnp.exp(draws), extent[dim] // shards_of).reshape((-1,) + (1,) * (len(extent) - 1 - dim))
    return level


def scatter_about(own_key, dims, scale, most, cuts=(), kind=jnp.bfloat16):
    values = jax.random.normal(own_key, dims, jnp.float32) * scale
    if len(cuts) > 0:
        values = block_levels(own_key, dims, cuts, -0.22, 0.18) * values
    return jnp.clip(values, min=-most, max=most).astype(kind)


def setup_inputs(seed: int = 0) -> dict:
    splits = jax.random.split(jax.random.key(seed), 6)
    query_rows = draw_query_rows(jax.random.fold_in(splits[5], 71), 0)
    out_grad = scatter_about(splits[1], (H, TOKENS, HD), 1.0, 6.0, ((1, 1024),))
    key_rows = draw_key_rows(jax.random.fold_in(splits[5], 71), 0)
    value_rows = scatter_about(splits[3], (H, KEYS, HD), 1.0, 6.0, ((1, 16),))
    routes = place_ends(jax.random.randint(splits[4], (N_BLK, N_BLK), 0, KBLOCKS), jax.random.fold_in(splits[4], 1), 0, KBLOCKS - 1).astype(jnp.int32)
    return {"query_rows": query_rows, "out_grad": out_grad, "key_rows": key_rows, "value_rows": value_rows, "routes": routes}


def reference(query_rows, out_grad, key_rows, value_rows, routes):
    group_length = TOK_DEV * N_ULYSSES
    key_stride = group_length // KG
    score_scale = 1.0 / math.sqrt(HD)
    group_ids = jnp.arange(N_BLK, dtype=jnp.int32)
    block_offsets = jnp.arange(KB, dtype=jnp.int32)
    own_offsets = jnp.arange(KG, dtype=jnp.int32)
    positions = jnp.arange(group_length, dtype=jnp.int32)

    def one_group(totals, group_index):
        key_total, value_total = totals
        queries = lax.dynamic_slice_in_dim(query_rows, group_index * group_length, group_length, 1).astype(jnp.float32)
        grad_rows = lax.dynamic_slice_in_dim(out_grad, group_index * group_length, group_length, 1).astype(jnp.float32)
        chosen = lax.dynamic_index_in_dim(routes, group_index, 0, keepdims=False).astype(jnp.int32)
        routed_ids = (group_ids[:, None] * KG + chosen[:, None] * KB + block_offsets[None, :]).reshape(-1)
        key_ids = jnp.concatenate([group_index * KG + own_offsets, routed_ids]).astype(jnp.int32)
        near_keys = jnp.take(key_rows, key_ids, axis=1).astype(jnp.float32)
        near_values = jnp.take(value_rows, key_ids, axis=1).astype(jnp.float32)
        own_visible = own_offsets[None, :] * key_stride <= positions[:, None]
        far_visible = jnp.broadcast_to(jnp.repeat(group_ids < group_index, KB)[None, :], (group_length, N_BLK * KB))
        visible = jnp.concatenate([own_visible, far_visible], axis=1)[None]
        scores = jnp.einsum('htd,hkd->htk', queries, near_keys) * score_scale
        row_max = lax.optimization_barrier(jnp.max(jnp.where(visible, scores, -jnp.inf), axis=-1, keepdims=True))
        expsum = jnp.where(visible, jnp.exp(scores - row_max), 0.0)
        weights = expsum / lax.optimization_barrier(jnp.sum(expsum, axis=-1, keepdims=True))
        weights_half = lax.optimization_barrier(weights.astype(jnp.bfloat16)).astype(jnp.float32)
        attended = jnp.einsum('htk,hkd->htd', weights_half, near_values)
        delta_rows = lax.optimization_barrier(jnp.sum(grad_rows * attended, axis=-1, keepdims=True))
        dweights = jnp.einsum('htd,hkd->htk', grad_rows, near_values)
        dscore = lax.optimization_barrier((weights * (dweights - delta_rows)).astype(jnp.bfloat16)).astype(jnp.float32)
        query_part = (jnp.einsum('htk,hkd->htd', dscore, near_keys) * score_scale).astype(jnp.bfloat16)
        split_score = dscore.reshape(H, N_ULYSSES, QS, TQB, NK)
        split_weight = weights_half.reshape(H, N_ULYSSES, QS, TQB, NK)
        split_query = queries.reshape(H, N_ULYSSES, QS, TQB, HD)
        split_grad = grad_rows.reshape(H, N_ULYSSES, QS, TQB, HD)
        key_part = jnp.einsum('husrk,husrd->shkd', split_score, split_query) * score_scale
        value_part = jnp.einsum('husrk,husrd->shkd', split_weight, split_grad)
        key_total = key_total.at[:, :, key_ids, :].add(key_part)
        value_total = value_total.at[:, :, key_ids, :].add(value_part)
        return ((key_total, value_total), query_part)
    zeros_total = jnp.zeros((QS, H, KEYS, HD), jnp.float32)
    (key_total, value_total), query_parts = lax.scan(one_group, (zeros_total, zeros_total), group_ids)
    query_grad = jnp.moveaxis(query_parts, 0, 1).reshape(H, TOKENS, HD)
    key_grad = lax.optimization_barrier(jnp.sum(lax.optimization_barrier(key_total.astype(jnp.bfloat16)).astype(jnp.float32), axis=0))
    value_grad = lax.optimization_barrier(jnp.sum(lax.optimization_barrier(value_total.astype(jnp.bfloat16)).astype(jnp.float32), axis=0))
    return (query_grad, key_grad, value_grad)
```

```python
import functools
import math

import jax
import jax.numpy as jnp
from jax import lax
from jax.experimental import pallas as pl
from jax.experimental.pallas import tpu as pltpu
from jax.sharding import PartitionSpec as P

KB = 16
MESH = pl.DeviceIdType.MESH
VMEM_LIMIT = 60 * 1024 * 1024


class Sizes:
    def __init__(self, heads, group_keys, head_dim, tokens, groups, ranks):
        self.heads, self.group_keys, self.dim, self.tokens = heads, group_keys, head_dim, tokens
        self.groups, self.ranks = groups, ranks
        self.half = groups // 2
        self.ny = group_keys // KB
        self.nz = ranks // self.ny
        self.part = heads // self.ny
        self.each = KB // self.nz
        self.units = 2 * self.part // self.nz
        self.major = self.ny // 2
        self.minor = self.ny - 1 - self.major
        self.own_rows = self.ny * self.each
        self.cross_rows = self.half * self.each
        self.stride = tokens * ranks // group_keys
        self.scale = 1.0 / math.sqrt(head_dim)


def where_am_i(sz):
    g = lax.axis_index("blk")
    r = lax.axis_index("ulysses")
    return g, r, g // sz.half, r // sz.nz, r % sz.nz


def greet(sz, g, r, y, z, whole_rows):
    barrier = pltpu.get_barrier_semaphore()
    count = 0
    for d in range(1, sz.groups):
        pl.semaphore_signal(
            barrier, inc=1, device_id=((g + d) % sz.groups, r), device_id_type=MESH
        )
        count += 1
    y_steps = range(1, sz.ny) if whole_rows else sorted({1, sz.ny - 1})
    for d in y_steps:
        pl.semaphore_signal(
            barrier,
            inc=1,
            device_id=(g, (y + d) % sz.ny * sz.nz + z),
            device_id_type=MESH,
        )
        count += 1
    for d in range(1, sz.nz):
        pl.semaphore_signal(
            barrier, inc=1, device_id=(g, y * sz.nz + (z + d) % sz.nz), device_id_type=MESH
        )
        count += 1
    pl.semaphore_wait(barrier, count)


def gather_kernel(
    sz,
    routes_ref,
    k_ref,
    v_ref,
    ft_ref,
    same_buf,
    cross_buf,
    same_send,
    same_recv,
    cross_send,
    cross_recv,
    z_send,
    z_recv,
    y_send,
    y_recv,
):
    g, r, zh, y, z = where_am_i(sz)
    gl = g - zh * sz.half
    half, ny, nz, part = sz.half, sz.ny, sz.nz, sz.part

    for jl in range(half):

        @pl.when(jl >= gl)
        def _(jl=jl):
            ft_ref[:, :, zh * half + jl] = jnp.zeros(
                (sz.heads, 2, KB, sz.dim), ft_ref.dtype
            )

    greet(sz, g, r, y, z, False)

    def cross_copy(i, q):
        u = z * sz.units + q
        return pltpu.make_async_remote_copy(
            src_ref=cross_buf.at[i, q],
            dst_ref=ft_ref.at[y * part + u // 2, u % 2, g],
            send_sem=cross_send.at[i, q],
            recv_sem=cross_recv.at[gl, q],
            device_id=(half + i, r),
            device_id_type=MESH,
        )

    def picker(count, target):
        shape = (count * KB, sz.group_keys)
        row = lax.broadcasted_iota(jnp.int32, shape, 0)
        col = lax.broadcasted_iota(jnp.int32, shape, 1)
        begin = jnp.zeros(shape, jnp.int32)
        for i in range(count):
            chosen = routes_ref[target(i) % sz.groups, g] * KB
            begin = jnp.where(row // KB == i, chosen, begin)
        return (col == begin + row % KB).astype(jnp.bfloat16)

    @pl.when(zh == 0)
    def _():
        pick = picker(half, lambda i: half + i)
        for q in range(sz.units):
            u = z * sz.units + q
            h = y * part + u // 2
            is_key = (u % 2 == 0).astype(jnp.float32)
            chosen = dot(pick, k_ref[h], 1, 0) * is_key + dot(pick, v_ref[h], 1, 0) * (1.0 - is_key)
            cross_buf[:, q] = chosen.astype(cross_buf.dtype).reshape(half, KB, sz.dim)
            for i in range(half):
                cross_copy(i, q).start()

    def same_copy(d):
        return pltpu.make_async_remote_copy(
            src_ref=same_buf.at[d - 1],
            dst_ref=ft_ref.at[:, :, g],
            send_sem=same_send.at[d - 1],
            recv_sem=same_recv.at[gl],
            device_id=(g + d, r),
            device_id_type=MESH,
        )

    if half > 1:
        pick_same = picker(half - 1, lambda i: g + 1 + i)

        def pick_head(h, _):
            for t, ref in ((0, k_ref), (1, v_ref)):
                chosen = dot(pick_same, ref[h], 1, 0).astype(same_buf.dtype)
                same_buf[:, h, t] = chosen.reshape(half - 1, KB, sz.dim)
            return 0

        lax.fori_loop(0, sz.heads, pick_head, 0)
    for d in range(1, half):

        @pl.when(gl + d < half)
        def _(d=d):
            same_copy(d).start()

    @pl.when(zh == 1)
    def _():
        def z_copy(d, q):
            u = z * sz.units + q
            piece = ft_ref.at[y * part + u // 2, u % 2, pl.ds(0, half)]
            return pltpu.make_async_remote_copy(
                src_ref=piece,
                dst_ref=piece,
                send_sem=z_send.at[d - 1, q],
                recv_sem=z_recv.at[z, q],
                device_id=(g, y * nz + (z + d) % nz),
                device_id_type=MESH,
            )

        def z_wait(d, q):
            src = (z + d) % nz
            u = src * sz.units + q
            piece = ft_ref.at[y * part + u // 2, u % 2, pl.ds(0, half)]
            pltpu.make_async_remote_copy(
                src_ref=piece,
                dst_ref=piece,
                send_sem=z_send.at[d - 1, q],
                recv_sem=z_recv.at[src, q],
                device_id=(g, y * nz + src),
                device_id_type=MESH,
            ).wait_recv()

        for q in range(sz.units):
            u = z * sz.units + q
            for i in range(half):
                dst = ft_ref.at[y * part + u // 2, u % 2, i]
                pltpu.make_async_remote_copy(
                    src_ref=dst,
                    dst_ref=dst,
                    send_sem=cross_send.at[i, q],
                    recv_sem=cross_recv.at[i, q],
                    device_id=(i, r),
                    device_id_type=MESH,
                ).wait_recv()
            for d in range(1, nz):
                z_copy(d, q).start()
        for q in range(sz.units):
            for d in range(1, nz):
                z_wait(d, q)

        def y_copy(p, slot, origin, sign):
            piece = ft_ref.at[origin % ny * part + p, :, pl.ds(0, half)]
            return pltpu.make_async_remote_copy(
                src_ref=piece,
                dst_ref=piece,
                send_sem=y_send.at[p, slot],
                recv_sem=y_recv.at[p, slot],
                device_id=(g, (y + sign + ny) % ny * nz + z),
                device_id_type=MESH,
            )

        for s in range(sz.major):

            def step(p, _, s=s):
                sign = 1 - 2 * (p % 2)
                if s > 0:
                    y_copy(p, s - 1, y - s * sign + ny, sign).wait_recv()
                y_copy(p, s, y - s * sign + ny, sign).start()
                if s < sz.minor:
                    if s > 0:
                        y_copy(p, sz.major + s - 1, y + s * sign + ny, sign).wait_recv()
                    y_copy(p, sz.major + s, y + s * sign + ny, -sign).start()
                return 0

            lax.fori_loop(0, part, step, 0)

        def last(p, _):
            sign = 1 - 2 * (p % 2)
            y_copy(p, sz.major - 1, y - sz.major * sign + ny, sign).wait_recv()
            if sz.minor > 0:
                y_copy(p, sz.major + sz.minor - 1, y + sz.minor * sign + ny, sign).wait_recv()
            for s in range(sz.major):
                y_copy(p, s, y - s * sign + ny, sign).wait_send()
            for s in range(sz.minor):
                y_copy(p, sz.major + s, y + s * sign + ny, -sign).wait_send()
            return 0

        lax.fori_loop(0, part, last, 0)
        for q in range(sz.units):
            for d in range(1, nz):
                z_copy(d, q).wait_send()

    @pl.when(zh == 0)
    def _():
        for i in range(half):
            for q in range(sz.units):
                cross_copy(i, q).wait_send()

    for d in range(1, half):

        @pl.when(gl + d < half)
        def _(d=d):
            same_copy(d).wait_send()

    for jl in range(half):

        @pl.when(jl < gl)
        def _(jl=jl):
            dst = ft_ref.at[:, :, zh * half + jl]
            pltpu.make_async_remote_copy(
                src_ref=dst,
                dst_ref=dst,
                send_sem=same_send.at[0],
                recv_sem=same_recv.at[jl],
                device_id=(zh * half + jl, r),
                device_id_type=MESH,
            ).wait_recv()


def gather_far(sz, routes, keys, values):
    vmem = pl.BlockSpec(memory_space=pltpu.VMEM)
    dma = pltpu.SemaphoreType.DMA
    return pl.pallas_call(
        functools.partial(gather_kernel, sz),
        out_shape=jax.ShapeDtypeStruct(
            (sz.heads, 2, sz.groups, KB, sz.dim), jnp.bfloat16
        ),
        in_specs=[pl.BlockSpec(memory_space=pltpu.SMEM), vmem, vmem],
        out_specs=vmem,
        scratch_shapes=[
            pltpu.VMEM((max(1, sz.half - 1), sz.heads, 2, KB, sz.dim), jnp.bfloat16),
            pltpu.VMEM((sz.half, sz.units, KB, sz.dim), jnp.bfloat16),
            dma((max(1, sz.half - 1),)),
            dma((sz.half,)),
            dma((sz.half, sz.units)),
            dma((sz.half, sz.units)),
            dma((max(1, sz.nz - 1), sz.units)),
            dma((sz.nz, sz.units)),
            dma((sz.part, sz.ny)),
            dma((sz.part, sz.ny)),
        ],
        compiler_params=pltpu.CompilerParams(
            collective_id=0, has_side_effects=True, vmem_limit_bytes=VMEM_LIMIT
        ),
        name="gather_far",
    )(routes, keys, values)


def order_matrix(blocks, each):
    count = blocks * KB
    row = lax.broadcasted_iota(jnp.int32, (count, count), 0)
    col = lax.broadcasted_iota(jnp.int32, (count, count), 1)
    rank = row // (blocks * each)
    block = row // each % blocks
    return (col == block * KB + rank * each + row % each).astype(jnp.bfloat16)


def dot(a, b, ca, cb):
    return lax.dot_general(a, b, (((ca,), (cb,)), ((), ())), preferred_element_type=jnp.float32)


def attend_kernel(sz, step_heads, q_ref, og_ref, k_ref, v_ref, ft_ref, dq_ref, px_ref, pc_ref, po_ref):
    g, r, zh, y, z = where_am_i(sz)
    gl = g - zh * sz.half
    half, ny, nz, each, dim = sz.half, sz.ny, sz.nz, sz.each, sz.dim
    n_own, n_far = sz.group_keys, half * KB
    own_order = order_matrix(ny, each)
    far_order = own_order if half == ny else order_matrix(half, each)
    row = lax.broadcasted_iota(jnp.int32, (n_own, sz.tokens), 0)
    tok = r * sz.tokens + lax.broadcasted_iota(jnp.int32, (n_own, sz.tokens), 1)
    key = row // each % ny * KB + row // (ny * each) * each + row % each
    far_row = lax.broadcasted_iota(jnp.int32, (n_far, sz.tokens), 0)
    visible = jnp.concatenate(
        [
            key * sz.stride <= tok,
            jnp.broadcast_to(zh == 1, (n_far, sz.tokens)),
            far_row // KB < gl,
        ],
        axis=0,
    )

    def one_head(i, _):
        q = q_ref[i]
        og = og_ref[i]

        def near(own_ref, t):
            own = dot(own_order, own_ref[i], 1, 0).astype(jnp.bfloat16)
            cross = ft_ref[i, t, pl.ds(0, half)].reshape(n_far, dim)
            cross = dot(far_order, cross, 1, 0).astype(jnp.bfloat16)
            same = ft_ref[i, t, pl.ds(zh * half, half)].reshape(n_far, dim)
            return jnp.concatenate([own, cross, same], axis=0)

        keys = near(k_ref, 0)
        values = near(v_ref, 1)
        scores = dot(keys, q, 1, 1) * sz.scale
        scores = jnp.where(visible, scores, -jnp.inf)
        e = jnp.exp(scores - jnp.max(scores, axis=0, keepdims=True))
        w = e / jnp.sum(e, axis=0, keepdims=True)
        wh = w.astype(jnp.bfloat16)
        dw = dot(values, og, 1, 1)
        delta = jnp.sum(wh.astype(jnp.float32) * dw, axis=0, keepdims=True)
        ds = (w * (dw - delta)).astype(jnp.bfloat16)
        dq_ref[i] = (dot(ds, keys, 0, 0) * sz.scale).astype(dq_ref.dtype)
        dk = dot(ds, q, 1, 0) * sz.scale
        dv = dot(wh, og, 1, 0)
        for t, part in ((0, dk), (1, dv)):
            po_ref[i, t] = part[:n_own].reshape(nz, sz.own_rows, dim)
            pc_ref[i, t] = part[n_own : n_own + n_far].astype(jnp.bfloat16).reshape(
                nz, sz.cross_rows, dim
            )
            px_ref[i, t] = part[n_own + n_far :].astype(jnp.bfloat16).reshape(half, KB, dim)
        return 0

    lax.fori_loop(0, step_heads, one_head, 0)


def attend(sz, query, grad, keys, values, far):
    step_heads = min(8, sz.heads)

    def spec(*dims):
        return pl.BlockSpec((step_heads,) + dims, lambda i: (i,) + (0,) * len(dims))

    shapes = [
        ((sz.tokens, sz.dim), jnp.bfloat16),
        ((2, sz.half, KB, sz.dim), jnp.bfloat16),
        ((2, sz.nz, sz.cross_rows, sz.dim), jnp.bfloat16),
        ((2, sz.nz, sz.own_rows, sz.dim), jnp.float32),
    ]
    return pl.pallas_call(
        functools.partial(attend_kernel, sz, step_heads),
        grid=(sz.heads // step_heads,),
        out_shape=[jax.ShapeDtypeStruct((sz.heads,) + s, d) for s, d in shapes],
        in_specs=[
            spec(sz.tokens, sz.dim),
            spec(sz.tokens, sz.dim),
            spec(sz.group_keys, sz.dim),
            spec(sz.group_keys, sz.dim),
            spec(2, sz.groups, KB, sz.dim),
        ],
        out_specs=[spec(*s) for s, _ in shapes],
        compiler_params=pltpu.CompilerParams(vmem_limit_bytes=VMEM_LIMIT),
        name="attend",
    )(query, grad, keys, values, far)


def reduce_kernel(
    sz,
    routes_ref,
    px_ref,
    pc_ref,
    po_ref,
    kg_ref,
    vg_ref,
    rx,
    ring_c,
    ring_o,
    out_c,
    out_o,
    tot,
    zs_c,
    zs_o,
    zr_c,
    zr_o,
    fin,
    xs,
    xr,
    os_,
    x_send,
    x_recv,
    y_send,
    y_recv,
    z_send,
    z_recv,
    c_send,
    c_recv,
    f_send,
    f_recv,
):
    g, r, zh, y, z = where_am_i(sz)
    gl = g - zh * sz.half
    half, ny, nz, part, each, dim = sz.half, sz.ny, sz.nz, sz.part, sz.each, sz.dim
    own_rows, cross_rows, heads = sz.own_rows, sz.cross_rows, sz.heads
    f32, bf16 = jnp.float32, jnp.bfloat16

    for i in range(half):

        @pl.when(i <= gl)
        def _(i=i):
            rx[:, :, i] = jnp.zeros((heads, 2, KB, dim), bf16)

    greet(sz, g, r, y, z, True)

    def x_copy(jl):
        return pltpu.make_async_remote_copy(
            src_ref=px_ref.at[:, :, jl],
            dst_ref=rx.at[:, :, gl],
            send_sem=x_send.at[jl],
            recv_sem=x_recv.at[gl],
            device_id=(zh * half + jl, r),
            device_id_type=MESH,
        )

    for jl in range(half - 1):

        @pl.when(jl < gl)
        def _(jl=jl):
            x_copy(jl).start()

    mix_shape = (sz.group_keys, half * KB)
    row = lax.broadcasted_iota(jnp.int32, mix_shape, 0)
    col = lax.broadcasted_iota(jnp.int32, mix_shape, 1)
    fits = (row // (ny * each) == col // each % nz) & (row % each == col % each)
    block = row // each % ny
    mix = jnp.zeros(mix_shape, f32)
    for i in range(half):
        chosen = fits & (col // KB == i) & (block == routes_ref[zh * half + i, g])
        mix = jnp.where(chosen, 1.0, mix)
    mix = mix.astype(bf16)

    def own_part(h, t):
        more = dot(mix, rx[h, t].reshape(half * KB, dim), 1, 0)
        return po_ref[h, t] + more.reshape(nz, own_rows, dim)

    def cross_part(h, t):
        return pc_ref[h, t].astype(f32)

    kinds = (
        (0, cross_part, ring_c, out_c, zs_c, zr_c, cross_rows),
        (1, own_part, ring_o, out_o, zs_o, zr_o, own_rows),
    )

    def y_copy(kind, p, slot, sign):
        return pltpu.make_async_remote_copy(
            src_ref=kind[3].at[p, slot],
            dst_ref=kind[2].at[p, slot],
            send_sem=y_send.at[kind[0], p, slot],
            recv_sem=y_recv.at[kind[0], p, slot],
            device_id=(g, (y + sign + ny) % ny * nz + z),
            device_id_type=MESH,
        )

    def z_copy(kind, p, d):
        to = (z + d) % nz
        return pltpu.make_async_remote_copy(
            src_ref=kind[4].at[p, to],
            dst_ref=kind[5].at[p, z],
            send_sem=z_send.at[kind[0], p, d],
            recv_sem=z_recv.at[kind[0], p, z],
            device_id=(g, y * nz + to),
            device_id_type=MESH,
        )

    def z_wait(kind, p, d):
        src = (z + d) % nz
        pltpu.make_async_remote_copy(
            src_ref=kind[4].at[p, src],
            dst_ref=kind[5].at[p, src],
            send_sem=z_send.at[kind[0], p, d],
            recv_sem=z_recv.at[kind[0], p, src],
            device_id=(g, y * nz + src),
            device_id_type=MESH,
        ).wait_recv()

    def ring_step(kind, s):
        _, mine, ring, out, zs, _, rows = kind

        def one(p, _):
            sign = 1 - 2 * (p % 2)
            ways = []
            if s < sz.major:
                ways.append((0, sign, y + (sz.major - s) * sign))
            if s < sz.minor:
                ways.append((sz.major, -sign, y - (sz.minor - s) * sign))
            for base, way, chunk in ways:
                h = (chunk + ny) % ny * part + p
                if s > 0:
                    y_copy(kind, p, base + s - 1, way).wait_recv()
                for t in range(2):
                    total = mine(h, t)
                    if s > 0:
                        total = total + ring[p, base + s - 1, t].astype(f32)
                    out[p, base + s, t] = total.astype(bf16)
                y_copy(kind, p, base + s, way).start()
            if s == sz.major:
                y_copy(kind, p, sz.major - 1, sign).wait_recv()
                if sz.minor > 0:
                    y_copy(kind, p, sz.major + sz.minor - 1, -sign).wait_recv()
                for t in range(2):
                    total = mine(y * part + p, t) + ring[p, sz.major - 1, t].astype(f32)
                    if sz.minor > 0:
                        total = total + ring[p, sz.major + sz.minor - 1, t].astype(f32)
                    zs[p, :, t] = total.astype(bf16)
                    tot[kind[0], p, t, :, pl.ds(0, rows)] = total
                for d in range(1, nz):
                    z_copy(kind, p, d).start()
            return 0

        lax.fori_loop(0, part, one, 0)

    def finish(kind, store):
        zr, rows = kind[5], kind[6]

        def one(p, _):
            for d in range(1, nz):
                z_wait(kind, p, d)
            for t in range(2):
                total = tot[kind[0], p, t, z, pl.ds(0, rows)]
                for d in range(1, nz):
                    total = total + zr[p, (z + d) % nz, t].astype(f32)
                fin[kind[0], t, pl.ds(0, rows)] = total
                store(p, t)
            return 0

        lax.fori_loop(0, part, one, 0)

    def c_copy(j):
        return pltpu.make_async_remote_copy(
            src_ref=xs.at[j],
            dst_ref=xr.at[gl],
            send_sem=c_send.at[j],
            recv_sem=c_recv.at[gl],
            device_id=(j, r),
            device_id_type=MESH,
        )

    def cross_step(s):
        @pl.when(zh == 1)
        def _():
            ring_step(kinds[0], s)

    cross_step(0)

    for i in range(1, half):

        @pl.when(i > gl)
        def _(i=i):
            pltpu.make_async_remote_copy(
                src_ref=px_ref.at[:, :, 0],
                dst_ref=rx.at[:, :, i],
                send_sem=x_send.at[0],
                recv_sem=x_recv.at[i],
                device_id=(zh * half + i, r),
                device_id_type=MESH,
            ).wait_recv()

    ring_step(kinds[1], 0)
    for s in range(1, sz.major + 1):
        cross_step(s)
        ring_step(kinds[1], s)

    @pl.when(zh == 1)
    def _():
        def store(p, t):
            for j in range(half):
                xs[j, t, p] = fin[0, t, pl.ds(j * each, each)]

        finish(kinds[0], store)
        for j in range(half):
            c_copy(j).start()

    def store_own(p, t):
        for b in range(ny):
            os_[b, t, p] = fin[1, t, pl.ds(b * each, each)]

    finish(kinds[1], store_own)

    @pl.when(zh == 0)
    def _():
        for i in range(half):
            pltpu.make_async_remote_copy(
                src_ref=xs.at[0],
                dst_ref=xr.at[i],
                send_sem=c_send.at[0],
                recv_sem=c_recv.at[i],
                device_id=(half + i, r),
                device_id_type=MESH,
            ).wait_recv()
        for b in range(ny):
            total = os_[b]
            for i in range(half):
                total = total + jnp.where(routes_ref[half + i, g] == b, xr[i], 0.0)
            os_[b] = total

    def f_copy(t, d):
        to = (y + d) % ny
        return pltpu.make_async_remote_copy(
            src_ref=os_.at[to, t],
            dst_ref=(kg_ref, vg_ref)[t].at[pl.ds(y * part, part)],
            send_sem=f_send.at[t, d],
            recv_sem=f_recv.at[t, y],
            device_id=(g, to * nz + z),
            device_id_type=MESH,
        )

    for d in range(1, ny):
        for t in range(2):
            f_copy(t, d).start()
    for t, ref in ((0, kg_ref), (1, vg_ref)):
        ref[pl.ds(y * part, part)] = os_[y, t]

    def sends(kind):
        def one(p, _):
            sign = 1 - 2 * (p % 2)
            for slot in range(ny - 1):
                y_copy(kind, p, slot, sign).wait_send()
            for d in range(1, nz):
                z_copy(kind, p, d).wait_send()
            return 0

        lax.fori_loop(0, part, one, 0)

    @pl.when(zh == 1)
    def _():
        sends(kinds[0])
        for j in range(half):
            c_copy(j).wait_send()

    sends(kinds[1])
    for jl in range(half - 1):

        @pl.when(jl < gl)
        def _(jl=jl):
            x_copy(jl).wait_send()

    for d in range(1, ny):
        src = (y + d) % ny
        for t in range(2):
            f_copy(t, d).wait_send()
            dst = (kg_ref, vg_ref)[t].at[pl.ds(src * part, part)]
            pltpu.make_async_remote_copy(
                src_ref=dst,
                dst_ref=dst,
                send_sem=f_send.at[t, d],
                recv_sem=f_recv.at[t, src],
                device_id=(g, src * nz + z),
                device_id_type=MESH,
            ).wait_recv()


def reduce_parts(sz, routes, px, pc, po):
    vmem = pl.BlockSpec(memory_space=pltpu.VMEM)
    dma = pltpu.SemaphoreType.DMA
    f32, bf16 = jnp.float32, jnp.bfloat16
    heads, half, ny, nz, part, each, dim = (
        sz.heads,
        sz.half,
        sz.ny,
        sz.nz,
        sz.part,
        sz.each,
        sz.dim,
    )
    own_rows, cross_rows = sz.own_rows, sz.cross_rows
    most = max(own_rows, cross_rows)
    out = jax.ShapeDtypeStruct((heads, each, dim), f32)
    return pl.pallas_call(
        functools.partial(reduce_kernel, sz),
        out_shape=[out, out],
        in_specs=[pl.BlockSpec(memory_space=pltpu.SMEM), vmem, vmem, vmem],
        out_specs=[vmem, vmem],
        scratch_shapes=[
            pltpu.VMEM((heads, 2, half, KB, dim), bf16),
            pltpu.VMEM((part, ny - 1, 2, nz, cross_rows, dim), bf16),
            pltpu.VMEM((part, ny - 1, 2, nz, own_rows, dim), bf16),
            pltpu.VMEM((part, ny - 1, 2, nz, cross_rows, dim), bf16),
            pltpu.VMEM((part, ny - 1, 2, nz, own_rows, dim), bf16),
            pltpu.VMEM((2, part, 2, nz, most, dim), f32),
            pltpu.VMEM((part, nz, 2, cross_rows, dim), bf16),
            pltpu.VMEM((part, nz, 2, own_rows, dim), bf16),
            pltpu.VMEM((part, nz, 2, cross_rows, dim), bf16),
            pltpu.VMEM((part, nz, 2, own_rows, dim), bf16),
            pltpu.VMEM((2, 2, most, dim), f32),
            pltpu.VMEM((half, 2, part, each, dim), f32),
            pltpu.VMEM((half, 2, part, each, dim), f32),
            pltpu.VMEM((ny, 2, part, each, dim), f32),
            dma((half,)),
            dma((half,)),
            dma((2, part, ny - 1)),
            dma((2, part, ny - 1)),
            dma((2, part, nz)),
            dma((2, part, nz)),
            dma((half,)),
            dma((half,)),
            dma((2, ny)),
            dma((2, ny)),
        ],
        compiler_params=pltpu.CompilerParams(
            collective_id=1, has_side_effects=True, vmem_limit_bytes=VMEM_LIMIT
        ),
        name="reduce_parts",
    )(routes, px, pc, po)


def solution(mesh):
    def body(query_rows, out_grad, key_rows, value_rows, routes):
        heads, tokens, dim = query_rows.shape
        sz = Sizes(
            heads, key_rows.shape[1], dim, tokens, mesh.shape["blk"], mesh.shape["ulysses"]
        )
        far = gather_far(sz, routes, key_rows, value_rows)
        query_grad, px, pc, po = attend(sz, query_rows, out_grad, key_rows, value_rows, far)
        key_grad, value_grad = reduce_parts(sz, routes, px, pc, po)
        return query_grad, key_grad, value_grad

    return jax.shard_map(
        body,
        mesh=mesh,
        in_specs=(
            P(None, ("blk", "ulysses"), None),
            P(None, ("blk", "ulysses"), None),
            P(None, "blk", None),
            P(None, "blk", None),
            P(),
        ),
        out_specs=(
            P(None, ("blk", "ulysses"), None),
            P(None, ("blk", "ulysses"), None),
            P(None, ("blk", "ulysses"), None),
        ),
        check_vma=False,
    )
```

```python
import functools
import math

import jax
import jax.numpy as jnp
from jax import lax
from jax.experimental import pallas as pl
from jax.experimental.pallas import tpu as pltpu
from jax.sharding import PartitionSpec as P

KB = 16
MESH = pl.DeviceIdType.MESH
VMEM_LIMIT = 60 * 1024 * 1024


class Sizes:
    def __init__(self, heads, group_keys, head_dim, tokens, groups, ranks):
        self.heads, self.group_keys, self.dim, self.tokens = heads, group_keys, head_dim, tokens
        self.groups, self.ranks = groups, ranks
        self.half = groups // 2
        self.ny = group_keys // KB
        self.nz = ranks // self.ny
        self.part = heads // self.ny
        self.each = KB // self.nz
        self.units = 2 * self.part // self.nz
        self.major = self.ny // 2
        self.minor = self.ny - 1 - self.major
        self.own_rows = self.ny * self.each
        self.stride = tokens * ranks // group_keys
        self.scale = 1.0 / math.sqrt(head_dim)


def where_am_i(sz):
    g = lax.axis_index("blk")
    r = lax.axis_index("ulysses")
    return g, r, g // sz.half, r // sz.nz, r % sz.nz


def greet(sz, g, r, zh, y, z):
    barrier = pltpu.get_barrier_semaphore()

    def signal(group, rank):
        pl.semaphore_signal(barrier, inc=1, device_id=(group, rank), device_id_type=MESH)

    for d in range(1, sz.groups):
        signal((g + d) % sz.groups, r)
    for d in range(1, sz.ny):
        signal(g, (y + d) % sz.ny * sz.nz + z)
    for d in range(1, sz.nz):
        signal(g, y * sz.nz + (z + d) % sz.nz)
    for i in range(sz.half):
        signal(zh * z + (1 - zh) * (sz.half + i), y * sz.nz + zh * i + (1 - zh) * g)
    pl.semaphore_wait(barrier, sz.groups + sz.ny + sz.nz + sz.half - 3)


def order_matrix(blocks, each):
    count = blocks * KB
    row = lax.broadcasted_iota(jnp.int32, (count, count), 0)
    col = lax.broadcasted_iota(jnp.int32, (count, count), 1)
    rank = row // (blocks * each)
    block = row // each % blocks
    return (col == block * KB + rank * each + row % each).astype(jnp.bfloat16)


def dot(a, b, ca, cb):
    return lax.dot_general(a, b, (((ca,), (cb,)), ((), ())), preferred_element_type=jnp.float32)


def kernel(
    sz,
    routes_ref,
    q_ref,
    og_ref,
    k_ref,
    v_ref,
    dq_ref,
    kg_ref,
    vg_ref,
    same_buf,
    cross_buf,
    fs,
    fc,
    kp,
    vp,
    bias,
    mix,
    px,
    pc,
    po,
    rx,
    ring_c,
    ring_o,
    out_c,
    out_o,
    tot,
    zs,
    zr,
    fin,
    xs,
    xr,
    os_,
    same_send,
    same_recv,
    cross_send,
    cross_recv,
    gz_send,
    gz_recv,
    gy_send,
    gy_recv,
    x_send,
    x_recv,
    y_send,
    y_recv,
    z_send,
    z_recv,
    c_send,
    c_recv,
    f_send,
    f_recv,
):
    g, r, zh, y, z = where_am_i(sz)
    gl = g - zh * sz.half
    half, ny, nz, part, each, dim = sz.half, sz.ny, sz.nz, sz.part, sz.each, sz.dim
    heads, major, minor, own_rows = sz.heads, sz.major, sz.minor, sz.own_rows
    n_own, n_far = sz.group_keys, half * KB
    f32, bf16 = jnp.float32, jnp.bfloat16

    def remote(src, dst, send_sem, recv_sem, group, rank):
        return pltpu.make_async_remote_copy(
            src_ref=src,
            dst_ref=dst,
            send_sem=send_sem,
            recv_sem=recv_sem,
            device_id=(group, rank),
            device_id_type=MESH,
        )

    greet(sz, g, r, zh, y, z)


    def cross_copy(i, n):
        u = z * sz.units + n
        return remote(
            cross_buf.at[i, n],
            fc.at[u // 2, y, u % 2, g],
            cross_send.at[i, n],
            cross_recv.at[gl, n],
            half + i,
            r,
        )

    def picker(count, target):
        shape = (count * KB, n_own)
        row = lax.broadcasted_iota(jnp.int32, shape, 0)
        col = lax.broadcasted_iota(jnp.int32, shape, 1)
        begin = jnp.zeros(shape, jnp.int32)
        for i in range(count):
            chosen = routes_ref[target(i) % sz.groups, g] * KB
            begin = jnp.where(row // KB == i, chosen, begin)
        return (col == begin + row % KB).astype(bf16)

    @pl.when(zh == 0)
    def _():
        pick = picker(half, lambda i: half + i)
        for n in range(sz.units):
            u = z * sz.units + n
            h = y * part + u // 2
            is_key = (u % 2 == 0).astype(f32)
            chosen = dot(pick, k_ref[h], 1, 0) * is_key + dot(pick, v_ref[h], 1, 0) * (1.0 - is_key)
            cross_buf[:, n] = chosen.astype(bf16).reshape(half, KB, dim)
            for i in range(half):
                cross_copy(i, n).start()

    def same_copy(p, d):
        return remote(
            same_buf.at[d - 1, p],
            fs.at[p, gl],
            same_send.at[p, d - 1],
            same_recv.at[p, gl],
            g + d,
            r,
        )

    if half > 1:
        pick_same = picker(half - 1, lambda i: g + 1 + i)

        def pick_part(p, _):
            def pick_head(c, _):
                for t, ref in ((0, k_ref), (1, v_ref)):
                    chosen = dot(pick_same, ref[c * part + p], 1, 0).astype(bf16)
                    same_buf[:, p, c, t] = chosen.reshape(half - 1, KB, dim)
                return 0

            lax.fori_loop(0, ny, pick_head, 0)
            for d in range(1, half):

                @pl.when(gl + d < half)
                def _(d=d):
                    same_copy(p, d).start()

            return 0

        lax.fori_loop(0, part, pick_part, 0)

    def gz_copy(d, n):
        u = z * sz.units + n
        piece = fc.at[u // 2, y, u % 2]
        return remote(
            piece,
            piece,
            gz_send.at[d - 1, n],
            gz_recv.at[z, n],
            g,
            y * nz + (z + d) % nz,
        )

    def gz_wait(d, n):
        src = (z + d) % nz
        u = src * sz.units + n
        piece = fc.at[u // 2, y, u % 2]
        remote(
            piece, piece, gz_send.at[d - 1, n], gz_recv.at[src, n], g, y * nz + src
        ).wait_recv()

    @pl.when(zh == 1)
    def _():
        for n in range(sz.units):
            u = z * sz.units + n
            for i in range(half):
                dst = fc.at[u // 2, y, u % 2, i]
                remote(dst, dst, cross_send.at[i, n], cross_recv.at[i, n], i, r).wait_recv()
            for d in range(1, nz):
                gz_copy(d, n).start()


    nothing = jnp.zeros((part, ny, 2, KB, dim), bf16)
    for i in range(half):

        @pl.when(i >= gl)
        def _(i=i):
            fs[:, i] = nothing

        @pl.when(i <= gl)
        def _(i=i):
            rx[:, i] = nothing

    @pl.when(zh == 0)
    def _():
        fc[...] = jnp.zeros((part, ny, 2, half, KB, dim), bf16)

    row = lax.broadcasted_iota(jnp.int32, (n_own, sz.tokens), 0)
    tok = r * sz.tokens + lax.broadcasted_iota(jnp.int32, (n_own, sz.tokens), 1)
    key = row // each % ny * KB + row // (ny * each) * each + row % each
    far_row = lax.broadcasted_iota(jnp.int32, (n_far, sz.tokens), 0)
    bias[pl.ds(0, n_own)] = jnp.where(key * sz.stride <= tok, 0.0, -jnp.inf)
    bias[pl.ds(n_own, n_far)] = jnp.where(far_row >= (1 - zh) * n_far, 0.0, -jnp.inf)
    bias[pl.ds(n_own + n_far, n_far)] = jnp.where(far_row // KB < gl, 0.0, -jnp.inf)

    mix_shape = (n_own, n_far)
    row = lax.broadcasted_iota(jnp.int32, mix_shape, 0)
    col = lax.broadcasted_iota(jnp.int32, mix_shape, 1)
    fits = (row // (ny * each) == col // each % nz) & (row % each == col % each)
    block = row // each % ny
    spots = jnp.zeros(mix_shape, f32)
    for i in range(half):
        chosen = fits & (col // KB == i) & (block == routes_ref[zh * half + i, g])
        spots = jnp.where(chosen, 1.0, spots)
    mix[...] = spots.astype(bf16)

    own_order = order_matrix(ny, each)

    def order_own(h, _):
        kp[h] = dot(own_order, k_ref[h], 1, 0).astype(bf16)
        vp[h] = dot(own_order, v_ref[h], 1, 0).astype(bf16)
        return 0

    lax.fori_loop(0, heads, order_own, 0)


    def gy_copy(p, slot, origin, way):
        piece = fc.at[p, (origin + ny) % ny]
        return remote(
            piece,
            piece,
            gy_send.at[p, slot],
            gy_recv.at[p, slot],
            g,
            (y + way + ny) % ny * nz + z,
        )

    @pl.when(zh == 1)
    def _():
        for n in range(sz.units):
            for d in range(1, nz):
                gz_wait(d, n)

        for s in range(major):

            def step(p, _, s=s):
                sign = 1 - 2 * (p % 2)
                if s > 0:
                    gy_copy(p, s - 1, y - s * sign, sign).wait_recv()
                gy_copy(p, s, y - s * sign, sign).start()
                if s < minor:
                    if s > 0:
                        gy_copy(p, major + s - 1, y + s * sign, -sign).wait_recv()
                    gy_copy(p, major + s, y + s * sign, -sign).start()
                return 0

            lax.fori_loop(0, part, step, 0)

    def far_is_here(p):
        sign = 1 - 2 * (p % 2)

        @pl.when(zh == 1)
        def _():
            gy_copy(p, major - 1, y - major * sign, sign).wait_recv()
            if minor > 0:
                gy_copy(p, major + minor - 1, y + minor * sign, -sign).wait_recv()

        for i in range(half - 1):

            @pl.when(i < gl)
            def _(i=i):
                dst = fs.at[p, i]
                remote(
                    dst, dst, same_send.at[p, 0], same_recv.at[p, i], zh * half + i, r
                ).wait_recv()


    log2e = math.log2(math.e)

    def attend(p, chunks):
        qs = [q_ref[c * part + p] for c in chunks]
        ogs = [og_ref[c * part + p] for c in chunks]

        def near(own, c, t):
            cross = fc[p, c, t].reshape(n_far, dim)
            same = fs[p, :, c, t].reshape(n_far, dim)
            return jnp.concatenate([own[c * part + p], cross, same], axis=0)

        keys = [near(kp, c, 0) for c in chunks]
        values = [near(vp, c, 1) for c in chunks]
        scores = [dot(k, q, 1, 1) * (sz.scale * log2e) + bias[...] for k, q in zip(keys, qs)]
        dws = [dot(v, og, 1, 1) for v, og in zip(values, ogs)]
        es = [jnp.exp2(x - jnp.max(x, axis=0, keepdims=True)) for x in scores]
        ws = [e * (1.0 / jnp.sum(e, axis=0, keepdims=True)) for e in es]
        whs = [w.astype(bf16) for w in ws]
        deltas = [
            jnp.sum(wh.astype(f32) * dw, axis=0, keepdims=True) for wh, dw in zip(whs, dws)
        ]
        dss = [
            (w * (dw - delta)).astype(bf16) for w, dw, delta in zip(ws, dws, deltas)
        ]
        for c, q, og, k, ds, wh in zip(chunks, qs, ogs, keys, dss, whs):
            dq_ref[c * part + p] = (dot(ds, k, 0, 0) * sz.scale).astype(dq_ref.dtype)
            dk = dot(ds, q, 1, 0) * sz.scale
            dv = dot(wh, og, 1, 0)
            for t, grad in ((0, dk), (1, dv)):
                po[p, c, t] = grad[:n_own].reshape(nz, own_rows, dim)
                pc[p, c, t] = grad[n_own : n_own + n_far].astype(bf16).reshape(half, KB, dim)
                px[p, :, c, t] = grad[n_own + n_far :].astype(bf16).reshape(half, KB, dim)


    def x_copy(p, jl):
        return remote(
            px.at[p, jl],
            rx.at[p, gl],
            x_send.at[p, jl],
            x_recv.at[p, gl],
            zh * half + jl,
            r,
        )

    def own_part(p, c, t):
        more = dot(mix[...], rx[p, :, c, t].reshape(n_far, dim), 1, 0)
        return po[p, c, t] + more.reshape(nz, own_rows, dim)

    def cross_part(p, c, t):
        return pc[p, c, t].astype(f32)

    cross = (0, cross_part, ring_c, out_c)
    own = (1, own_part, ring_o, out_o)

    def y_copy(kind, p, slot, way):
        return remote(
            kind[3].at[p, slot],
            kind[2].at[p, slot],
            y_send.at[kind[0], p, slot],
            y_recv.at[kind[0], p, slot],
            g,
            (y + way + ny) % ny * nz + z,
        )

    def ring_step(kind, p, s):
        sign = 1 - 2 * (p % 2)

        def hop(base, way, c):
            c = (c + ny) % ny

            @pl.when(s == 0)
            def _():
                for t in range(2):
                    kind[3][p, base, t] = kind[1](p, c, t).astype(bf16)

            @pl.when(s > 0)
            def _():
                y_copy(kind, p, base + s - 1, way).wait_recv()
                for t in range(2):
                    total = kind[1](p, c, t) + kind[2][p, base + s - 1, t].astype(f32)
                    kind[3][p, base + s, t] = total.astype(bf16)

            y_copy(kind, p, base + s, way).start()

        hop(0, sign, y + (major - s) * sign)
        if minor > 0:

            @pl.when(s < minor)
            def _():
                hop(major, -sign, y - (minor - s) * sign)

    def z_copy(kind, p, d):
        to = (z + d) % nz
        return remote(
            zs.at[kind[0], p, to],
            zr.at[kind[0], p, z],
            z_send.at[kind[0], p, d],
            z_recv.at[kind[0], p, z],
            g,
            y * nz + to,
        )

    def ring_end(kind, p):
        sign = 1 - 2 * (p % 2)
        ring = kind[2]
        y_copy(kind, p, major - 1, sign).wait_recv()
        if minor > 0:
            y_copy(kind, p, major + minor - 1, -sign).wait_recv()
        for t in range(2):
            total = kind[1](p, y, t) + ring[p, major - 1, t].astype(f32)
            if minor > 0:
                total = total + ring[p, major + minor - 1, t].astype(f32)
            zs[kind[0], p, :, t] = total.astype(bf16)
            tot[kind[0], p, t] = total
        for d in range(1, nz):
            z_copy(kind, p, d).start()

    def finish(kind, p, store):
        for d in range(1, nz):
            src = (z + d) % nz
            remote(
                zs.at[kind[0], p, src],
                zr.at[kind[0], p, src],
                z_send.at[kind[0], p, d],
                z_recv.at[kind[0], p, src],
                g,
                y * nz + src,
            ).wait_recv()
        for t in range(2):
            total = tot[kind[0], p, t, z]
            for d in range(1, nz):
                total = total + zr[kind[0], p, (z + d) % nz, t].astype(f32)
            fin[kind[0], t] = total
            store(p, t)

    def store_cross(p, t):
        for c in range(nz):
            xs[c, t, p] = fin[0, t, pl.ds(c * each, each)]

    def store_own(p, t):
        for b in range(ny):
            os_[b, t, p] = fin[1, t, pl.ds(b * each, each)]

    def c_copy(c):
        return remote(xs.at[c], xr.at[gl], c_send.at[c], c_recv.at[gl], z, y * nz + c)

    late = min(2, major - 1)

    def turn(it, _):
        p = it // major
        s = it % major
        sign = 1 - 2 * (p % 2)

        @pl.when(p < part)
        def _():
            @pl.when(s == 0)
            def _():
                far_is_here(p)

            attend(
                p,
                [
                    (y + (major - s) * sign + ny) % ny,
                    (y - (minor - s) * sign + ny) % ny,
                ],
            )

            @pl.when(s == major - 1)
            def _():
                for jl in range(half - 1):

                    @pl.when(jl < gl)
                    def _(jl=jl):
                        x_copy(p, jl).start()

            @pl.when(zh == 1)
            def _():
                ring_step(cross, p, s)

        @pl.when(p >= 1)
        def _():
            @pl.when((s == 0) & (zh == 1))
            def _():
                ring_end(cross, p - 1)

            @pl.when(s == 0)
            def _():
                for i in range(1, half):

                    @pl.when(i > gl)
                    def _(i=i):
                        dst = rx.at[p - 1, i]
                        remote(
                            dst, dst, x_send.at[p - 1, 0], x_recv.at[p - 1, i], zh * half + i, r
                        ).wait_recv()

            ring_step(own, p - 1, s)

            @pl.when((s == late) & (zh == 1))
            def _():
                finish(cross, p - 1, store_cross)

                @pl.when(p == part)
                def _():
                    for c in range(nz):
                        c_copy(c).start()

        @pl.when(p >= 2)
        def _():
            @pl.when(s == 0)
            def _():
                ring_end(own, p - 2)

            @pl.when(s == late)
            def _():
                finish(own, p - 2, store_own)

        return 0

    lax.fori_loop(0, (part + 1) * major, turn, 0)
    ring_end(own, part - 1)
    finish(own, part - 1, store_own)

    @pl.when(zh == 0)
    def _():
        for i in range(half):
            remote(
                xs.at[0], xr.at[i], c_send.at[0], c_recv.at[i], half + i, y * nz + g
            ).wait_recv()
        for b in range(ny):
            total = os_[b]
            for i in range(half):
                total = total + jnp.where(routes_ref[half + i, g] == b, xr[i], 0.0)
            os_[b] = total

    def f_copy(t, d):
        to = (y + d) % ny
        return remote(
            os_.at[to, t],
            (kg_ref, vg_ref)[t].at[pl.ds(y * part, part)],
            f_send.at[t, d],
            f_recv.at[t, y],
            g,
            to * nz + z,
        )

    for d in range(1, ny):
        for t in range(2):
            f_copy(t, d).start()
    for t, ref in ((0, kg_ref), (1, vg_ref)):
        ref[pl.ds(y * part, part)] = os_[y, t]


    def sends(kind):
        def one(p, _):
            sign = 1 - 2 * (p % 2)
            for slot in range(ny - 1):
                y_copy(kind, p, slot, sign).wait_send()
            for d in range(1, nz):
                z_copy(kind, p, d).wait_send()
            return 0

        lax.fori_loop(0, part, one, 0)

    @pl.when(zh == 0)
    def _():
        for i in range(half):
            for n in range(sz.units):
                cross_copy(i, n).wait_send()

    @pl.when(zh == 1)
    def _():
        def ring_left(p, _):
            for slot in range(ny - 1):
                gy_copy(p, slot, y, 1).wait_send()
            return 0

        lax.fori_loop(0, part, ring_left, 0)
        for n in range(sz.units):
            for d in range(1, nz):
                gz_copy(d, n).wait_send()
        sends(cross)
        for c in range(nz):
            c_copy(c).wait_send()

    sends(own)

    def straight(p, _):
        for d in range(1, half):

            @pl.when(gl + d < half)
            def _(d=d):
                same_copy(p, d).wait_send()

        for jl in range(half - 1):

            @pl.when(jl < gl)
            def _(jl=jl):
                x_copy(p, jl).wait_send()

        return 0

    lax.fori_loop(0, part, straight, 0)

    for d in range(1, ny):
        src = (y + d) % ny
        for t in range(2):
            f_copy(t, d).wait_send()
            dst = (kg_ref, vg_ref)[t].at[pl.ds(src * part, part)]
            remote(
                dst, dst, f_send.at[t, d], f_recv.at[t, src], g, src * nz + z
            ).wait_recv()


def backward(sz, routes, query, grad, keys, values):
    vmem = pl.BlockSpec(memory_space=pltpu.VMEM)
    dma = pltpu.SemaphoreType.DMA
    f32, bf16 = jnp.float32, jnp.bfloat16
    heads, half, ny, nz, part, each, dim, own_rows = (
        sz.heads,
        sz.half,
        sz.ny,
        sz.nz,
        sz.part,
        sz.each,
        sz.dim,
        sz.own_rows,
    )
    near = sz.group_keys + 2 * half * KB
    small = jax.ShapeDtypeStruct((heads, each, dim), f32)
    ring_c = pltpu.VMEM((part, ny - 1, 2, half, KB, dim), bf16)
    ring_o = pltpu.VMEM((part, ny - 1, 2, nz, own_rows, dim), bf16)
    return pl.pallas_call(
        functools.partial(kernel, sz),
        out_shape=[jax.ShapeDtypeStruct((heads, sz.tokens, dim), bf16), small, small],
        in_specs=[pl.BlockSpec(memory_space=pltpu.SMEM), vmem, vmem, vmem, vmem],
        out_specs=[vmem, vmem, vmem],
        scratch_shapes=[
            pltpu.VMEM((max(1, half - 1), part, ny, 2, KB, dim), bf16),
            pltpu.VMEM((half, sz.units, KB, dim), bf16),
            pltpu.VMEM((part, half, ny, 2, KB, dim), bf16),
            pltpu.VMEM((part, ny, 2, half, KB, dim), bf16),
            pltpu.VMEM((heads, sz.group_keys, dim), bf16),
            pltpu.VMEM((heads, sz.group_keys, dim), bf16),
            pltpu.VMEM((near, sz.tokens), f32),
            pltpu.VMEM((sz.group_keys, half * KB), bf16),
            pltpu.VMEM((part, half, ny, 2, KB, dim), bf16),
            pltpu.VMEM((part, ny, 2, half, KB, dim), bf16),
            pltpu.VMEM((part, ny, 2, nz, own_rows, dim), f32),
            pltpu.VMEM((part, half, ny, 2, KB, dim), bf16),
            ring_c,
            ring_o,
            ring_c,
            ring_o,
            pltpu.VMEM((2, part, 2, nz, KB, dim), f32),
            pltpu.VMEM((2, part, nz, 2, KB, dim), bf16),
            pltpu.VMEM((2, part, nz, 2, KB, dim), bf16),
            pltpu.VMEM((2, 2, KB, dim), f32),
            pltpu.VMEM((nz, 2, part, each, dim), f32),
            pltpu.VMEM((half, 2, part, each, dim), f32),
            pltpu.VMEM((ny, 2, part, each, dim), f32),
            dma((part, max(1, half - 1))),
            dma((part, half)),
            dma((half, sz.units)),
            dma((half, sz.units)),
            dma((max(1, nz - 1), sz.units)),
            dma((nz, sz.units)),
            dma((part, ny)),
            dma((part, ny)),
            dma((part, half)),
            dma((part, half)),
            dma((2, part, ny - 1)),
            dma((2, part, ny - 1)),
            dma((2, part, nz)),
            dma((2, part, nz)),
            dma((nz,)),
            dma((half,)),
            dma((2, ny)),
            dma((2, ny)),
        ],
        compiler_params=pltpu.CompilerParams(
            collective_id=0, has_side_effects=True, vmem_limit_bytes=VMEM_LIMIT
        ),
        name="backward",
    )(routes, query, grad, keys, values)


def solution(mesh):
    def body(query_rows, out_grad, key_rows, value_rows, routes):
        heads, tokens, dim = query_rows.shape
        sz = Sizes(
            heads, key_rows.shape[1], dim, tokens, mesh.shape["blk"], mesh.shape["ulysses"]
        )
        assert sz.half == sz.nz and sz.own_rows == KB
        return backward(sz, routes, query_rows, out_grad, key_rows, value_rows)

    return jax.shard_map(
        body,
        mesh=mesh,
        in_specs=(
            P(None, ("blk", "ulysses"), None),
            P(None, ("blk", "ulysses"), None),
            P(None, "blk", None),
            P(None, "blk", None),
            P(),
        ),
        out_specs=(
            P(None, ("blk", "ulysses"), None),
            P(None, ("blk", "ulysses"), None),
            P(None, ("blk", "ulysses"), None),
        ),
        check_vma=False,
    )
```
